32 devices in a mesh: section: 4 (over y, x), dp: 2 (over core), tp: 4 (over z).
Axes of the slice: x: 2, y: 2, z: 4, core: 2. Of those that a mesh axis runs over, the one named last changes fastest.
Arguments:
- enc_kv: bfloat16 [2, 2, 4, 256, 3072], P('dp', None, 'tp', 'section'), as said below
- queries: bfloat16 [2, 4, 512, 3072], P('dp', 'section', None, 'tp'), as said below
- grad_out: bfloat16 [2, 4, 512, 3072], P('dp', 'section', None, 'tp'), may hold values from -6 to 6
- plan: int32 [2, 4], P('dp'), may hold values from 0 to 3
- enc_lengths: int32 [2, 4], P('dp'), may hold values from 32 to 256
- tgt_lengths: int32 [2, 4], P('dp'), may hold values from 64 to 512
Outputs:
- attended: bfloat16 [2, 4, 512, 3072], P('dp', 'section', None, 'tp')
- grad_queries: bfloat16 [2, 4, 512, 3072], P('dp', 'section', None, 'tp')
- grad_enc_kv: bfloat16 [2, 2, 4, 256, 3072], P('dp', None, 'tp', 'section')
The draws below stay inside these ranges and needn't reach their ends.
Inputs may be any that keep to these rules, and one draw needn't show every extreme that they name: `enc_kv`: entries lie within -5.5 to 5.5. `queries`: entries lie within -5.5 to 5.5.
All inputs are finite; a program needn't handle non-finite values.
Results may differ from the reference program's by a relative error of at most 0.0084.
Values may be sent and summed in bfloat16 or wider, within the bound.
No kernel may reach another device: no remote copies, remote signals or barrier semaphores. Data moves between devices by JAX's collectives and lax.ppermute only.
A program may use at most 64 MiB of HBM per device.

```python
import jax
import jax.numpy as jnp
from jax import lax

HEADS = 24
HEAD_DIM = 128
TGT = 512
MB = 4
ENC = 256
HH = 3072
N_SECTION = 4
N_DP = 2


def draw_enc_kv(key, part):
    shape = (N_DP, 2, MB, ENC, HEADS * HEAD_DIM)
    noise_key = jax.random.fold_in(key, 11)
    values = jnp.clip(jax.random.normal(noise_key, shape, jnp.float32), -5.5, 5.5)
    return values.astype(jnp.bfloat16)


def draw_queries(key, part):
    shape = (N_DP, N_SECTION, TGT, HEADS * HEAD_DIM)
    noise_key = jax.random.fold_in(key, 13)
    values = jnp.clip(jax.random.normal(noise_key, shape, jnp.float32), -5.5, 5.5)
    return values.astype(jnp.bfloat16)


def ragged_lengths(key, longest):
    drawn = jax.random.randint(jax.random.fold_in(key, 3), (N_DP, MB), longest // 8, longest + 1, dtype=jnp.int32)
    chosen = jax.random.randint(jax.random.fold_in(key, 5), (), 0, N_DP * MB, dtype=jnp.int32)
    flat_index = jnp.arange(N_DP * MB, dtype=jnp.int32).reshape(N_DP, MB)
    return jnp.where(flat_index == chosen, longest, drawn).astype(jnp.int32)


def draw_enc_lengths(key, part):
    return ragged_lengths(jax.random.fold_in(key, 41), ENC)


def draw_tgt_lengths(key, part):
    return ragged_lengths(jax.random.fold_in(key, 43), TGT)


def touch_ends(entries, key, least, top_value):
    longest = entries.shape.index(max(entries.shape))
    spots = []
    for shift in (0, 1):
        where = [jax.random.randint(jax.random.fold_in(key, axis), (), 0, length) for axis, length in enumerate(entries.shape)]
        where[longest] = (where[longest] + shift) % entries.shape[longest]
        spots.append(tuple(where))
    return entries.at[spots[0]].set(least).at[spots[1]].set(top_value)


def block_levels(rng, extent, split, least, high):
    def one(dim, parts):
        draws = jax.random.uniform(jax.random.fold_in(jax.random.fold_in(rng, 6), dim), (parts,), jnp.float32, least / len(split), high / len(split))
        return jnp.repeat(jnp.exp(draws), extent[dim] // parts).reshape((-1,) + (1,) * (len(extent) - dim - 1))

    factor_of = one(*split[0])
    for cut in split[1:]:
        factor_of = factor_of * one(*cut)
    return factor_of


def gaussian(key, extent, width, limit, cuts=(), kind=jnp.bfloat16):
    array = width * jax.random.normal(key, extent, jnp.float32)
    if cuts:
        array = array * block_levels(key, extent, cuts, -0.22, 0.18)
    return jnp.clip(array, -limit, limit).astype(kind)


def setup_inputs(seed: int = 0) -> dict:
    key_of = jax.random.split(jax.random.key(seed), 7)
    return {
        "enc_kv": draw_enc_kv(jax.random.fold_in(key_of[6], 71), 0),
        "queries": draw_queries(jax.random.fold_in(key_of[6], 71), 0),
        "grad_out": gaussian(key_of[2], (N_DP, N_SECTION, TGT, HH), 1.0, 6.0, ((0, 2), (1, 4), (3, 4))),
        "plan": touch_ends(jax.random.randint(key_of[3], (N_DP, N_SECTION), 0, MB), jax.random.fold_in(key_of[3], 1), 0, MB - 1).astype(jnp.int32),
        "enc_lengths": draw_enc_lengths(jax.random.fold_in(key_of[6], 71), 0),
        "tgt_lengths": draw_tgt_lengths(jax.random.fold_in(key_of[6], 71), 0),
    }


def head_pass(query_rows, key_rows, value_rows, grad_rows, key_len, query_len):
    scaling = query_rows.shape[-1] ** -0.5
    scores = jnp.dot(query_rows, key_rows.T, preferred_element_type=jnp.float32) * scaling
    key_valid = jnp.arange(key_rows.shape[0], dtype=jnp.int32) < key_len
    scores = jnp.where(key_valid[None, :], scores, -jnp.inf)
    row_top = jnp.max(scores, axis=-1, keepdims=True)
    expon = jnp.exp(scores - row_top)
    probs_full = expon / jnp.sum(expon, axis=-1, keepdims=True)
    probs_half = probs_full.astype(jnp.bfloat16)
    query_valid = (jnp.arange(query_rows.shape[0], dtype=jnp.int32) < query_len)[:, None]
    context = jnp.dot(probs_half, value_rows, preferred_element_type=jnp.float32)
    attended = jnp.where(query_valid, context, 0.0).astype(jnp.bfloat16)
    masked_grad = jnp.where(query_valid, grad_rows, jnp.zeros_like(grad_rows))
    grad_value = jnp.dot(probs_half.T, masked_grad, preferred_element_type=jnp.float32).astype(jnp.bfloat16)
    grad_probs = jnp.dot(masked_grad, value_rows.T, preferred_element_type=jnp.float32)
    row_dot = jnp.sum(probs_full * grad_probs, axis=-1, keepdims=True)
    grad_scores = (probs_full * (grad_probs - row_dot)).astype(jnp.bfloat16)
    grad_query = (jnp.dot(grad_scores, key_rows, preferred_element_type=jnp.float32) * scaling).astype(jnp.bfloat16)
    grad_key = (jnp.dot(grad_scores.T, query_rows, preferred_element_type=jnp.float32) * scaling).astype(jnp.bfloat16)
    return attended, grad_query, grad_key, grad_value


def all_heads(query_block, key_block, value_block, grad_block, key_len, query_len):
    head_count = query_block.shape[1] // HEAD_DIM

    def split_heads(stacked):
        return stacked.reshape(stacked.shape[0], head_count, HEAD_DIM).transpose(1, 0, 2)

    def join_heads(stacked):
        return stacked.transpose(1, 0, 2).reshape(stacked.shape[1], head_count * HEAD_DIM)

    def run_one(pieces):
        return head_pass(pieces[0], pieces[1], pieces[2], pieces[3], key_len, query_len)

    attended, grad_query, grad_key, grad_value = lax.map(
        run_one, (split_heads(query_block), split_heads(key_block), split_heads(value_block), split_heads(grad_block)))
    return join_heads(attended), join_heads(grad_query), join_heads(grad_key), join_heads(grad_value)


def reference(enc_kv, queries, grad_out, plan, enc_lengths, tgt_lengths):
    def one_replica(inputs):
        memory, query_set, grad_set, timetable, enc_len, tgt_len = inputs

        def one_section(section_inputs):
            query_block, grad_block, micro_id = section_inputs
            attended, grad_query, grad_key, grad_value = all_heads(
                query_block, memory[0, micro_id], memory[1, micro_id], grad_block,
                enc_len[micro_id], tgt_len[micro_id])
            return attended, grad_query, jnp.stack([grad_key, grad_value])

        attended, grad_query, grad_memory = lax.map(one_section, (query_set, grad_set, timetable))
        onehot = (timetable[:, None] == jnp.arange(MB, dtype=jnp.int32)[None, :]).astype(jnp.float32)
        summed = jnp.einsum("sm,skeh->kmeh", onehot, grad_memory.astype(jnp.float32))
        return attended, grad_query, summed.astype(jnp.bfloat16)

    attended, grad_queries, grad_enc_kv = lax.map(
        one_replica, (enc_kv, queries, grad_out, plan, enc_lengths, tgt_lengths))
    return attended, grad_queries, grad_enc_kv
```

```python
import functools
import math

import jax
import jax.numpy as jnp
from jax import lax
from jax.experimental import pallas as pl
from jax.experimental.pallas import tpu as pltpu
from jax.sharding import PartitionSpec as P

HEAD_DIM = 128
CHUNKS = 3

SMEM = pl.BlockSpec(memory_space=pltpu.SMEM)
VMEM = pl.BlockSpec(memory_space=pltpu.VMEM)
ANY = pl.BlockSpec(memory_space=pl.ANY)


def ahead(index, step, count):
    return lax.rem(index + step, count)


def behind(index, step, count):
    return lax.rem(index + count - step, count)


def shift(piece, axis, count, step):
    return lax.ppermute(piece, axis, [(i, (i + step) % count) for i in range(count)])


def near(array):
    return pltpu.with_memory_space_constraint(array, pltpu.VMEM)


def split_kernel(tp_count, chunks, width, head_cols, memory_ref, *outs):
    me = lax.axis_index("tp")
    for chunk in range(chunks):
        for step in range(tp_count):
            start = ahead(me, step, tp_count) * head_cols + chunk * width
            outs[chunk * tp_count + step][...] = memory_ref[:, :, pl.ds(pl.multiple_of(start, 128), width)]


def pick_kernel(tp_count, section_count, plan_ref, *refs):
    pieces, outs = refs[:tp_count], refs[tp_count:]
    me, tp_me = lax.axis_index("section"), lax.axis_index("tp")
    for step in range(section_count):
        micro = plan_ref[0, ahead(me, step, section_count)]
        back = behind(tp_me, micro, tp_count)
        for which in range(tp_count):

            @pl.when(back == which)
            def _():
                outs[step][...] = pieces[which][...]


def heads_kernel(section_count, chunk, width, plan_ref, key_len_ref, query_len_ref, query_ref, grad_ref, *refs):
    blocks = refs[:section_count]
    refs = refs[section_count:]
    if len(refs) > section_count + 2:
        refs = refs[2:]
    attended_ref, grad_query_ref = refs[:2]
    outs = refs[2:]
    me = lax.axis_index("section")
    micro = plan_ref[0, me]
    key_len, query_len = key_len_ref[0, micro], query_len_ref[0, micro]
    block_len = blocks[0].shape[1]
    tgt = query_ref.shape[0]
    scaling = HEAD_DIM ** (-0.5)
    row = lax.broadcasted_iota(jnp.int32, (block_len, tgt), 0)
    query_valid = lax.broadcasted_iota(jnp.int32, (tgt, HEAD_DIM), 0) < query_len
    nt = (((1,), (1,)), ((), ()))
    tn = (((0,), (0,)), ((), ()))
    for head in range(width // HEAD_DIM):
        cols = slice(head * HEAD_DIM, (head + 1) * HEAD_DIM)
        wide = slice(chunk * width + head * HEAD_DIM, chunk * width + (head + 1) * HEAD_DIM)
        query = query_ref[:, wide]
        grad = jnp.where(query_valid, grad_ref[:, wide], jnp.zeros((), jnp.bfloat16))
        keys = jnp.concatenate([block[0, :, cols] for block in blocks], axis=0)
        values = jnp.concatenate([block[1, :, cols] for block in blocks], axis=0)
        scores = lax.dot_general(keys, query, nt, preferred_element_type=jnp.float32) * scaling
        masked = []
        for step in range(section_count):
            left = key_len - behind(me, step, section_count) * block_len
            part = scores[step * block_len : (step + 1) * block_len]
            masked.append(jnp.where(row < left, part, -jnp.inf))
        scores = jnp.concatenate(masked, axis=0)
        top = jnp.max(scores, axis=0, keepdims=True)
        expon = jnp.exp(scores - top)
        probs = expon * (1.0 / jnp.sum(expon, axis=0, keepdims=True))
        half = probs.astype(jnp.bfloat16)
        context = lax.dot_general(half, values, tn, preferred_element_type=jnp.float32)
        attended_ref[:, wide] = jnp.where(query_valid, context, 0.0).astype(jnp.bfloat16)
        grad_value = jnp.dot(half, grad, preferred_element_type=jnp.float32).astype(jnp.bfloat16)
        grad_probs = lax.dot_general(values, grad, nt, preferred_element_type=jnp.float32)
        row_dot = jnp.sum(probs * grad_probs, axis=0, keepdims=True)
        grad_scores = (probs * (grad_probs - row_dot)).astype(jnp.bfloat16)
        grad_query = lax.dot_general(grad_scores, keys, tn, preferred_element_type=jnp.float32)
        grad_query_ref[:, wide] = (grad_query * scaling).astype(jnp.bfloat16)
        grad_key = jnp.dot(grad_scores, query, preferred_element_type=jnp.float32) * scaling
        grad_key = grad_key.astype(jnp.bfloat16)
        for step in range(section_count):
            rows = slice(step * block_len, (step + 1) * block_len)
            outs[step][0, :, cols] = grad_key[rows]
            outs[step][1, :, cols] = grad_value[rows]


def sum_kernel(tp_count, section_count, plan_ref, *refs):
    pieces, outs = refs[:section_count], refs[section_count:]
    me, tp_me = lax.axis_index("section"), lax.axis_index("tp")
    for step in range(tp_count):
        micro = ahead(tp_me, step, tp_count)
        total = jnp.zeros(outs[step].shape, jnp.float32)
        for back in range(section_count):
            weight = jnp.where(plan_ref[0, ahead(me, back, section_count)] == micro, 1.0, 0.0)
            total = total + weight * pieces[back][...].astype(jnp.float32)
        outs[step][...] = total.astype(jnp.bfloat16)


def join_kernel(tp_count, chunks, width, head_cols, *refs):
    pieces, out_ref = refs[:-1], refs[-1]
    me = lax.axis_index("tp")
    for chunk in range(chunks):
        for step in range(tp_count):
            start = behind(me, step, tp_count) * head_cols + chunk * width
            out_ref[:, :, pl.ds(pl.multiple_of(start, 128), width)] = pieces[chunk * tp_count + step][...]


def body(enc_kv, queries, grad_out, plan, enc_lengths, tgt_lengths):
    section_count = lax.axis_size("section")
    tp_count = lax.axis_size("tp")
    memory = enc_kv[0, :, 0]
    query, grad = queries[0, 0], grad_out[0, 0]
    block_len, columns = memory.shape[1:]
    tgt, head_cols = query.shape
    heads = head_cols // HEAD_DIM
    chunks = math.gcd(CHUNKS, heads)
    width = head_cols // chunks
    piece = pltpu.VMEM((2, block_len, width), jnp.bfloat16)
    rows = pltpu.VMEM((tgt, head_cols), jnp.bfloat16)
    params = pltpu.CompilerParams(vmem_limit_bytes=16 * 1024 * 1024)

    split = pl.pallas_call(
        functools.partial(split_kernel, tp_count, chunks, width, head_cols),
        out_shape=[piece] * (tp_count * chunks),
        in_specs=[VMEM],
        out_specs=[VMEM] * (tp_count * chunks),
        compiler_params=params,
        name="split",
    )(memory)

    query, grad = near(query), near(grad)
    arrived = []
    for chunk in range(chunks):
        parts = split[chunk * tp_count : (chunk + 1) * tp_count]
        parts = [parts[0]] + [shift(parts[step], "tp", tp_count, step) for step in range(1, tp_count)]
        picked = pl.pallas_call(
            functools.partial(pick_kernel, tp_count, section_count),
            out_shape=[piece] * section_count,
            in_specs=[SMEM] + [VMEM] * tp_count,
            out_specs=[VMEM] * section_count,
            compiler_params=params,
            name=f"pick{chunk}",
        )(plan, *map(near, parts))
        arrived.append(
            [picked[0]] + [shift(picked[step], "section", section_count, step) for step in range(1, section_count)]
        )

    results = []
    grads = []
    for chunk in range(chunks):
        done = pl.pallas_call(
            functools.partial(heads_kernel, section_count, chunk, width),
            out_shape=[rows, rows] + [piece] * section_count,
            in_specs=[SMEM] * 3 + [VMEM] * (2 + section_count + len(results)),
            out_specs=[VMEM] * (2 + section_count),
            input_output_aliases={5 + section_count + i: i for i in range(len(results))},
            compiler_params=params,
            name=f"heads{chunk}",
        )(plan, enc_lengths, tgt_lengths, query, grad, *map(near, arrived[chunk]), *map(near, results))
        results = list(done[:2])
        grads.append(done[2:])

    joined = []
    for chunk in range(chunks):
        pieces = grads[chunk]
        pieces = [pieces[0]] + [
            shift(pieces[step], "section", section_count, section_count - step) for step in range(1, section_count)
        ]
        summed = pl.pallas_call(
            functools.partial(sum_kernel, tp_count, section_count),
            out_shape=[piece] * tp_count,
            in_specs=[SMEM] + [VMEM] * section_count,
            out_specs=[VMEM] * tp_count,
            compiler_params=params,
            name=f"sum{chunk}",
        )(plan, *map(near, pieces))
        joined += [summed[0]] + [shift(summed[step], "tp", tp_count, step) for step in range(1, tp_count)]
    grad_memory = pl.pallas_call(
        functools.partial(join_kernel, tp_count, chunks, width, head_cols),
        out_shape=jax.ShapeDtypeStruct((2, block_len, columns), jnp.bfloat16),
        in_specs=[VMEM] * len(joined),
        out_specs=VMEM,
        compiler_params=params,
        name="join",
    )(*map(near, joined))
    return (results[0][None, None], results[1][None, None], grad_memory[None, :, None])


def solution(mesh):
    in_specs = (
        P("dp", None, "tp", "section", None),
        P("dp", "section", None, "tp"),
        P("dp", "section", None, "tp"),
        P("dp", None),
        P("dp", None),
        P("dp", None),
    )
    out_specs = (
        P("dp", "section", None, "tp"),
        P("dp", "section", None, "tp"),
        P("dp", None, "tp", "section", None),
    )
    return jax.shard_map(body, mesh=mesh, in_specs=in_specs, out_specs=out_specs, check_vma=False)
```

```python
import functools
import math

import jax
import jax.numpy as jnp
from jax import lax
from jax.experimental import pallas as pl
from jax.experimental.pallas import tpu as pltpu
from jax.sharding import PartitionSpec as P

HEAD_DIM = 128
CHUNKS = 2

SMEM = pl.BlockSpec(memory_space=pltpu.SMEM)
VMEM = pl.BlockSpec(memory_space=pltpu.VMEM)
ANY = pl.BlockSpec(memory_space=pl.ANY)


def ahead(index, step, count):
    return lax.rem(index + step, count)


def behind(index, step, count):
    return lax.rem(index + count - step, count)


def shift(piece, axis, count, step):
    return lax.ppermute(piece, axis, [(i, (i + step) % count) for i in range(count)])


def near(array):
    return pltpu.with_memory_space_constraint(array, pltpu.VMEM)


def split_kernel(tp_count, chunks, width, head_cols, plan_ref, key_len_ref, query_len_ref, memory_ref, facts_ref, *outs):
    me = lax.axis_index("tp")
    section_count = plan_ref.shape[1]
    for section in range(section_count):
        facts_ref[section] = plan_ref[0, section]
    micro = plan_ref[0, lax.axis_index("section")]
    facts_ref[section_count] = key_len_ref[0, micro]
    facts_ref[section_count + 1] = query_len_ref[0, micro]
    for chunk in range(chunks):
        for step in range(tp_count):
            start = ahead(me, step, tp_count) * head_cols + chunk * width
            outs[chunk * tp_count + step][...] = memory_ref[:, :, pl.ds(pl.multiple_of(start, 128), width)]


def pick_kernel(tp_count, section_count, facts_ref, *refs):
    pieces, outs = refs[:tp_count], refs[tp_count:]
    me, tp_me = lax.axis_index("section"), lax.axis_index("tp")
    for step in range(section_count):
        micro = facts_ref[ahead(me, step, section_count)]
        back = behind(tp_me, micro, tp_count)
        for which in range(tp_count):

            @pl.when(back == which)
            def _():
                outs[step][...] = pieces[which][...]


def heads_kernel(section_count, chunk, width, facts_ref, query_ref, grad_ref, *refs):
    blocks = refs[:section_count]
    attended_ref, grad_query_ref, *outs = refs[-2 - section_count :]
    me = lax.axis_index("section")
    key_len, query_len = facts_ref[section_count], facts_ref[section_count + 1]
    block_len = blocks[0].shape[1]
    tgt = query_ref.shape[0]
    scaling = HEAD_DIM ** (-0.5)
    scaling_two = scaling * math.log2(math.e)
    row = lax.broadcasted_iota(jnp.int32, (block_len, 1), 0)
    lefts = [key_len - behind(me, step, section_count) * block_len for step in range(section_count)]
    bias = jnp.concatenate([jnp.where(row < left, 0.0, -jnp.inf) for left in lefts], axis=0)
    query_valid = lax.broadcasted_iota(jnp.int32, (tgt, HEAD_DIM), 0) < query_len
    nt = (((1,), (1,)), ((), ()))
    tn = (((0,), (0,)), ((), ()))
    none = jnp.zeros((), jnp.bfloat16)
    for head in range(width // HEAD_DIM):
        cols = slice(head * HEAD_DIM, (head + 1) * HEAD_DIM)
        wide = slice(chunk * width + head * HEAD_DIM, chunk * width + (head + 1) * HEAD_DIM)
        query = query_ref[:, wide]
        grad = jnp.where(query_valid, grad_ref[:, wide], none)
        keys = jnp.concatenate([block[0, :, cols] for block in blocks], axis=0)
        values = jnp.concatenate([block[1, :, cols] for block in blocks], axis=0)
        scores = lax.dot_general(keys, query, nt, preferred_element_type=jnp.float32) + bias
        top = jnp.max(scores, axis=0, keepdims=True)
        expon = jnp.exp2((scores - top) * scaling_two)
        probs = expon * (1.0 / jnp.sum(expon, axis=0, keepdims=True))
        half = probs.astype(jnp.bfloat16)
        grad_probs = lax.dot_general(values, grad, nt, preferred_element_type=jnp.float32)
        row_dot = jnp.sum(probs * grad_probs, axis=0, keepdims=True)
        grad_scores = (probs * (grad_probs - row_dot)).astype(jnp.bfloat16)
        grad_value = jnp.dot(half, grad, preferred_element_type=jnp.float32).astype(jnp.bfloat16)
        grad_key = jnp.dot(grad_scores, query, preferred_element_type=jnp.float32) * scaling
        grad_key = grad_key.astype(jnp.bfloat16)
        context = lax.dot_general(values, half, tn, preferred_element_type=jnp.float32).astype(jnp.bfloat16).T
        attended_ref[:, wide] = jnp.where(query_valid, context, none)
        grad_query = lax.dot_general(keys, grad_scores, tn, preferred_element_type=jnp.float32) * scaling
        grad_query_ref[:, wide] = grad_query.astype(jnp.bfloat16).T
        for step in range(section_count):
            rows = slice(step * block_len, (step + 1) * block_len)
            outs[step][0, :, cols] = grad_key[rows]
            outs[step][1, :, cols] = grad_value[rows]


def sum_kernel(tp_count, section_count, facts_ref, *refs):
    pieces, outs = refs[:section_count], refs[section_count:]
    me, tp_me = lax.axis_index("section"), lax.axis_index("tp")
    for step in range(tp_count):
        micro = ahead(tp_me, step, tp_count)
        total = jnp.zeros(outs[step].shape, jnp.float32)
        for back in range(section_count):
            weight = jnp.where(facts_ref[ahead(me, back, section_count)] == micro, 1.0, 0.0)
            total = total + weight * pieces[back][...].astype(jnp.float32)
        outs[step][...] = total.astype(jnp.bfloat16)


def join_kernel(tp_count, chunks, width, head_cols, *refs):
    pieces, out_ref = refs[:-1], refs[-1]
    me = lax.axis_index("tp")
    for chunk in range(chunks):
        for step in range(tp_count):
            start = behind(me, step, tp_count) * head_cols + chunk * width
            out_ref[:, :, pl.ds(pl.multiple_of(start, 128), width)] = pieces[chunk * tp_count + step][...]


def body(enc_kv, queries, grad_out, plan, enc_lengths, tgt_lengths):
    section_count = lax.axis_size("section")
    tp_count = lax.axis_size("tp")
    memory = enc_kv[0, :, 0]
    query, grad = queries[0, 0], grad_out[0, 0]
    block_len, columns = memory.shape[1:]
    tgt, head_cols = query.shape
    heads = head_cols // HEAD_DIM
    chunks = math.gcd(CHUNKS, heads)
    width = head_cols // chunks
    piece = pltpu.VMEM((2, block_len, width), jnp.bfloat16)
    rows = pltpu.VMEM((tgt, head_cols), jnp.bfloat16)
    params = pltpu.CompilerParams(vmem_limit_bytes=16 * 1024 * 1024)

    facts, *split = pl.pallas_call(
        functools.partial(split_kernel, tp_count, chunks, width, head_cols),
        out_shape=[pltpu.SMEM((section_count + 2,), jnp.int32)] + [piece] * (tp_count * chunks),
        in_specs=[SMEM] * 3 + [VMEM],
        out_specs=[SMEM] + [VMEM] * (tp_count * chunks),
        compiler_params=params,
        name="split",
    )(plan, enc_lengths, tgt_lengths, memory)
    facts = pltpu.with_memory_space_constraint(facts, pltpu.SMEM)

    query, grad = near(query), near(grad)
    arrived = []
    for chunk in range(chunks):
        parts = split[chunk * tp_count : (chunk + 1) * tp_count]
        parts = [parts[0]] + [shift(parts[step], "tp", tp_count, step) for step in range(1, tp_count)]
        picked = pl.pallas_call(
            functools.partial(pick_kernel, tp_count, section_count),
            out_shape=[piece] * section_count,
            in_specs=[SMEM] + [VMEM] * tp_count,
            out_specs=[VMEM] * section_count,
            compiler_params=params,
            name=f"pick{chunk}",
        )(facts, *map(near, parts))
        arrived.append(
            [picked[0]] + [shift(picked[step], "section", section_count, step) for step in range(1, section_count)]
        )

    results, returned, gate = [], [], []
    for chunk in range(chunks):
        done = pl.pallas_call(
            functools.partial(heads_kernel, section_count, chunk, width),
            out_shape=[rows, rows] + [piece] * section_count,
            in_specs=[SMEM] + [VMEM] * (2 + section_count + len(results) + len(gate)),
            out_specs=[VMEM] * (2 + section_count),
            input_output_aliases={3 + section_count + i: i for i in range(len(results))},
            compiler_params=params,
            cost_estimate=pl.CostEstimate(
                flops=12 * tgt * block_len * section_count * width, bytes_accessed=12 * 1024 * 1024 // chunks * 2, transcendentals=0
            ),
            name=f"heads{chunk}",
        )(facts, query, grad, *map(near, arrived[chunk]), *map(near, results), *map(near, gate))
        results = list(done[:2])
        returned.append(
            [done[2]]
            + [shift(done[2 + step], "section", section_count, section_count - step) for step in range(1, section_count)]
        )
        gate = returned[chunk][1:2]

    joined = []
    for chunk in range(chunks):
        pieces = returned[chunk]
        summed = pl.pallas_call(
            functools.partial(sum_kernel, tp_count, section_count),
            out_shape=[piece] * tp_count,
            in_specs=[SMEM] + [VMEM] * section_count,
            out_specs=[VMEM] * tp_count,
            compiler_params=params,
            name=f"sum{chunk}",
        )(facts, *map(near, pieces))
        joined += [summed[0]] + [shift(summed[step], "tp", tp_count, step) for step in range(1, tp_count)]
    grad_memory = pl.pallas_call(
        functools.partial(join_kernel, tp_count, chunks, width, head_cols),
        out_shape=jax.ShapeDtypeStruct((2, block_len, columns), jnp.bfloat16),
        in_specs=[VMEM] * len(joined),
        out_specs=VMEM,
        compiler_params=params,
        name="join",
    )(*map(near, joined))
    return (results[0][None, None], results[1][None, None], grad_memory[None, :, None])


def solution(mesh):
    in_specs = (
        P("dp", None, "tp", "section", None),
        P("dp", "section", None, "tp"),
        P("dp", "section", None, "tp"),
        P("dp", None),
        P("dp", None),
        P("dp", None),
    )
    out_specs = (
        P("dp", "section", None, "tp"),
        P("dp", "section", None, "tp"),
        P("dp", None, "tp", "section", None),
    )
    return jax.shard_map(body, mesh=mesh, in_specs=in_specs, out_specs=out_specs, check_vma=False)
```

```python
import functools
import math

import jax
import jax.numpy as jnp
from jax import lax
from jax.experimental import pallas as pl
from jax.experimental.pallas import tpu as pltpu
from jax.sharding import PartitionSpec as P

HEAD_DIM = 128
CHUNKS = 2

SMEM = pl.BlockSpec(memory_space=pltpu.SMEM)
VMEM = pl.BlockSpec(memory_space=pltpu.VMEM)
ANY = pl.BlockSpec(memory_space=pl.ANY)


def ahead(index, step, count):
    return lax.rem(index + step, count)


def behind(index, step, count):
    return lax.rem(index + count - step, count)


def swap(piece, step, count):
    return lax.ppermute(piece, "section", [(i, i ^ step) for i in range(count)])


def shift(piece, step, count):
    return lax.ppermute(piece, "tp", [(i, (i + step) % count) for i in range(count)])


def near(array):
    return pltpu.with_memory_space_constraint(array, pltpu.VMEM)


def columns_of(chunk, width, head_cols, owner):
    return pl.ds(pl.multiple_of(owner * head_cols + chunk * width, 128), width)


def run_copies(pairs, sem):
    copies = [pltpu.make_async_copy(source, target, sem.at[i]) for i, (source, target) in enumerate(pairs)]
    for copy in copies:
        copy.start()
    for copy in copies:
        copy.wait()


def split_kernel(tp_count, chunk, width, head_cols, memory_ref, *refs):
    me = lax.axis_index("tp")
    outs, sem = refs[:-1], refs[-1]
    owners = [ahead(me, step, tp_count) for step in range(tp_count)]
    run_copies([(memory_ref.at[:, :, columns_of(chunk, width, head_cols, o)], out) for o, out in zip(owners, outs)], sem)


def facts_kernel(section_count, plan_ref, key_len_ref, query_len_ref, facts_ref):
    for section in range(section_count):
        facts_ref[section] = plan_ref[0, section]
    micro = plan_ref[0, lax.axis_index("section")]
    facts_ref[section_count] = key_len_ref[0, micro]
    facts_ref[section_count + 1] = query_len_ref[0, micro]


def pick_kernel(tp_count, steps, facts_ref, *refs):
    pieces, outs = refs[:tp_count], refs[-len(steps) :]
    me, tp_me = lax.axis_index("section"), lax.axis_index("tp")
    for step, out_ref in zip(steps, outs):
        back = behind(tp_me, facts_ref[me ^ step], tp_count)
        for which in range(tp_count):

            @pl.when(back == which)
            def _():
                out_ref[...] = pieces[which][...]


def heads_kernel(section_count, chunk, width, facts_ref, query_ref, grad_ref, *refs):
    blocks = refs[:section_count]
    attended_ref, grad_query_ref, *outs = refs[-2 - section_count :]
    me = lax.axis_index("section")
    key_len, query_len = facts_ref[section_count], facts_ref[section_count + 1]
    block_len = blocks[0].shape[1]
    tgt = query_ref.shape[0]
    scaling = HEAD_DIM ** (-0.5)
    scaling_two = scaling * math.log2(math.e)
    row = lax.broadcasted_iota(jnp.int32, (block_len, 1), 0)
    lefts = [key_len - (me ^ step) * block_len for step in range(section_count)]
    bias = jnp.concatenate([jnp.where(row < left, 0.0, -jnp.inf) for left in lefts], axis=0)
    query_valid = lax.broadcasted_iota(jnp.int32, (tgt, HEAD_DIM), 0) < query_len
    nt = (((1,), (1,)), ((), ()))
    tn = (((0,), (0,)), ((), ()))
    none = jnp.zeros((), jnp.bfloat16)
    for head in range(width // HEAD_DIM):
        cols = slice(head * HEAD_DIM, (head + 1) * HEAD_DIM)
        wide = slice(chunk * width + head * HEAD_DIM, chunk * width + (head + 1) * HEAD_DIM)
        query = query_ref[:, wide]
        grad = jnp.where(query_valid, grad_ref[:, wide], none)
        keys = jnp.concatenate([block[0, :, cols] for block in blocks], axis=0)
        values = jnp.concatenate([block[1, :, cols] for block in blocks], axis=0)
        scores = lax.dot_general(keys, query, nt, preferred_element_type=jnp.float32) + bias
        top = jnp.max(scores, axis=0, keepdims=True)
        expon = jnp.exp2((scores - top) * scaling_two)
        probs = expon * (1.0 / jnp.sum(expon, axis=0, keepdims=True))
        half = probs.astype(jnp.bfloat16)
        grad_probs = lax.dot_general(values, grad, nt, preferred_element_type=jnp.float32)
        row_dot = jnp.sum(probs * grad_probs, axis=0, keepdims=True)
        grad_scores = (probs * (grad_probs - row_dot)).astype(jnp.bfloat16)
        grad_value = jnp.dot(half, grad, preferred_element_type=jnp.float32).astype(jnp.bfloat16)
        grad_key = jnp.dot(grad_scores, query, preferred_element_type=jnp.float32) * scaling
        grad_key = grad_key.astype(jnp.bfloat16)
        context = lax.dot_general(values, half, tn, preferred_element_type=jnp.float32).astype(jnp.bfloat16).T
        attended_ref[:, wide] = jnp.where(query_valid, context, none)
        grad_query = lax.dot_general(keys, grad_scores, tn, preferred_element_type=jnp.float32) * scaling
        grad_query_ref[:, wide] = grad_query.astype(jnp.bfloat16).T
        for step in range(section_count):
            rows = slice(step * block_len, (step + 1) * block_len)
            outs[step][0, :, cols] = grad_key[rows]
            outs[step][1, :, cols] = grad_value[rows]


def sum_kernel(tp_count, section_count, facts_ref, *refs):
    pieces, outs = refs[:section_count], refs[section_count:]
    me, tp_me = lax.axis_index("section"), lax.axis_index("tp")
    for step in range(tp_count):
        micro = ahead(tp_me, step, tp_count)
        total = jnp.zeros(outs[step].shape, jnp.float32)
        for back in range(section_count):
            weight = jnp.where(facts_ref[me ^ back] == micro, 1.0, 0.0)
            total = total + weight * pieces[back][...].astype(jnp.float32)
        outs[step][...] = total.astype(jnp.bfloat16)


def join_kernel(tp_count, chunk, width, head_cols, *refs):
    pieces, out_ref, sem = refs[:tp_count], refs[-2], refs[-1]
    me = lax.axis_index("tp")
    owners = [behind(me, step, tp_count) for step in range(tp_count)]
    run_copies([(piece, out_ref.at[:, :, columns_of(chunk, width, head_cols, o)]) for o, piece in zip(owners, pieces)], sem)


def body(enc_kv, queries, grad_out, plan, enc_lengths, tgt_lengths):
    section_count = lax.axis_size("section")
    tp_count = lax.axis_size("tp")
    memory = enc_kv[0, :, 0]
    query, grad = queries[0, 0], grad_out[0, 0]
    block_len, columns = memory.shape[1:]
    tgt, head_cols = query.shape
    heads = head_cols // HEAD_DIM
    chunks = math.gcd(CHUNKS, heads)
    width = head_cols // chunks
    piece = pltpu.VMEM((2, block_len, width), jnp.bfloat16)
    rows = pltpu.VMEM((tgt, head_cols), jnp.bfloat16)
    params = pltpu.CompilerParams(vmem_limit_bytes=16 * 1024 * 1024)

    memory = pltpu.with_memory_space_constraint(memory, pltpu.HBM)
    copy_sem = pltpu.SemaphoreType.DMA((tp_count,))
    parts = []
    for chunk in range(chunks):
        split = pl.pallas_call(
            functools.partial(split_kernel, tp_count, chunk, width, head_cols),
            out_shape=[piece] * tp_count,
            in_specs=[ANY],
            out_specs=[VMEM] * tp_count,
            scratch_shapes=[copy_sem],
            compiler_params=params,
            name=f"split{chunk}",
        )(memory)
        parts.append([split[0]] + [shift(split[step], step, tp_count) for step in range(1, tp_count)])
    facts = pl.pallas_call(
        functools.partial(facts_kernel, section_count),
        out_shape=pltpu.SMEM((section_count + 2,), jnp.int32),
        in_specs=[SMEM] * 3,
        out_specs=SMEM,
        compiler_params=params,
        name="facts",
    )(plan, enc_lengths, tgt_lengths)
    facts = pltpu.with_memory_space_constraint(facts, pltpu.SMEM)

    def pick(chunk, steps, gate):
        return pl.pallas_call(
            functools.partial(pick_kernel, tp_count, steps),
            out_shape=[piece] * len(steps),
            in_specs=[SMEM] + [VMEM] * (tp_count + len(gate)),
            out_specs=[VMEM] * len(steps),
            compiler_params=params,
            name=f"pick{chunk}",
        )(facts, *map(near, parts[chunk]), *map(near, gate))

    query, grad = near(query), near(grad)
    results, returned = [], []
    steps = list(range(section_count))
    for chunk in range(chunks):
        if chunk == 0:
            picked = pick(chunk, steps, [])
        else:
            picked = pick(chunk, steps[:-1], []) + pick(chunk, steps[-1:], [returned[-1][0]])
        arrived = [picked[0]] + [swap(picked[step], step, section_count) for step in steps[1:]]
        done = pl.pallas_call(
            functools.partial(heads_kernel, section_count, chunk, width),
            out_shape=[rows, rows] + [piece] * section_count,
            in_specs=[SMEM] + [VMEM] * (2 + section_count + len(results)),
            out_specs=[VMEM] * (2 + section_count),
            input_output_aliases={3 + section_count + i: i for i in range(len(results))},
            compiler_params=params,
            cost_estimate=pl.CostEstimate(
                flops=12 * tgt * block_len * section_count * width, bytes_accessed=8 * 2**20, transcendentals=0
            ),
            name=f"heads{chunk}",
        )(facts, query, grad, *map(near, arrived), *map(near, results))
        results = list(done[:2])
        returned.append([done[2]] + [swap(done[2 + step], step, section_count) for step in steps[1:]])

    whole = []
    for chunk in range(chunks):
        summed = pl.pallas_call(
            functools.partial(sum_kernel, tp_count, section_count),
            out_shape=[piece] * tp_count,
            in_specs=[SMEM] + [VMEM] * section_count,
            out_specs=[VMEM] * tp_count,
            compiler_params=params,
            name=f"sum{chunk}",
        )(facts, *map(near, returned[chunk]))
        pieces = [summed[0]] + [shift(summed[step], step, tp_count) for step in range(1, tp_count)]
        whole = [
            pl.pallas_call(
                functools.partial(join_kernel, tp_count, chunk, width, head_cols),
                out_shape=pltpu.HBM((2, block_len, columns), jnp.bfloat16),
                in_specs=[VMEM] * tp_count + [ANY] * len(whole),
                out_specs=ANY,
                scratch_shapes=[copy_sem],
                input_output_aliases={tp_count: 0} if whole else {},
                compiler_params=params,
                name=f"join{chunk}",
            )(*map(near, pieces), *whole)
        ]
    return (results[0][None, None], results[1][None, None], whole[0][None, :, None])


def solution(mesh):
    in_specs = (
        P("dp", None, "tp", "section", None),
        P("dp", "section", None, "tp"),
        P("dp", "section", None, "tp"),
        P("dp", None),
        P("dp", None),
        P("dp", None),
    )
    out_specs = (
        P("dp", "section", None, "tp"),
        P("dp", "section", None, "tp"),
        P("dp", None, "tp", "section", None),
    )
    return jax.shard_map(body, mesh=mesh, in_specs=in_specs, out_specs=out_specs, check_vma=False)
```

```python
import functools
import math

import jax
import jax.numpy as jnp
from jax import lax
from jax.experimental import pallas as pl
from jax.experimental.pallas import tpu as pltpu
from jax.sharding import PartitionSpec as P

HEAD_DIM = 128
CHUNKS = 2

SMEM = pl.BlockSpec(memory_space=pltpu.SMEM)
VMEM = pl.BlockSpec(memory_space=pltpu.VMEM)
ANY = pl.BlockSpec(memory_space=pl.ANY)


def ahead(index, step, count):
    return lax.rem(index + step, count)


def behind(index, step, count):
    return lax.rem(index + count - step, count)


def swap(piece, step, count):
    return lax.ppermute(piece, "section", [(i, i ^ step) for i in range(count)])


def shift(piece, step, count):
    return lax.ppermute(piece, "tp", [(i, (i + step) % count) for i in range(count)])


def near(array):
    return pltpu.with_memory_space_constraint(array, pltpu.VMEM)


def columns_of(chunk, width, head_cols, owner):
    return pl.ds(pl.multiple_of(owner * head_cols + chunk * width, 128), width)


def run_copies(pairs, sem):
    copies = [pltpu.make_async_copy(source, target, sem.at[i]) for i, (source, target) in enumerate(pairs)]
    for copy in copies:
        copy.start()
    for copy in copies:
        copy.wait()


def split_kernel(tp_count, chunk, width, head_cols, memory_ref, *refs):
    me = lax.axis_index("tp")
    outs, sem = refs[-1 - tp_count : -1], refs[-1]
    owners = [ahead(me, step, tp_count) for step in range(tp_count)]
    run_copies([(memory_ref.at[:, :, columns_of(chunk, width, head_cols, o)], out) for o, out in zip(owners, outs)], sem)


def facts_kernel(section_count, plan_ref, key_len_ref, query_len_ref, facts_ref):
    for section in range(section_count):
        facts_ref[section] = plan_ref[0, section]
    micro = plan_ref[0, lax.axis_index("section")]
    facts_ref[section_count] = key_len_ref[0, micro]
    facts_ref[section_count + 1] = query_len_ref[0, micro]


def pick_kernel(tp_count, steps, facts_ref, *refs):
    pieces, outs = refs[:tp_count], refs[-len(steps) :]
    me, tp_me = lax.axis_index("section"), lax.axis_index("tp")
    for step, out_ref in zip(steps, outs):
        back = behind(tp_me, facts_ref[me ^ step], tp_count)
        for which in range(tp_count):

            @pl.when(back == which)
            def _():
                out_ref[...] = pieces[which][...]


def heads_kernel(section_count, chunk, width, facts_ref, query_ref, grad_ref, *refs):
    blocks = refs[:section_count]
    attended_ref, grad_query_ref, *outs = refs[-2 - section_count :]
    me = lax.axis_index("section")
    key_len, query_len = facts_ref[section_count], facts_ref[section_count + 1]
    block_len = blocks[0].shape[1]
    tgt = query_ref.shape[0]
    scaling = HEAD_DIM ** (-0.5)
    scaling_two = scaling * math.log2(math.e)
    row = lax.broadcasted_iota(jnp.int32, (block_len, 1), 0)
    lefts = [key_len - (me ^ step) * block_len for step in range(section_count)]
    bias = jnp.concatenate([jnp.where(row < left, 0.0, -jnp.inf) for left in lefts], axis=0)
    query_valid = lax.broadcasted_iota(jnp.int32, (tgt, HEAD_DIM), 0) < query_len
    nt = (((1,), (1,)), ((), ()))
    tn = (((0,), (0,)), ((), ()))
    none = jnp.zeros((), jnp.bfloat16)
    for head in range(width // HEAD_DIM):
        cols = slice(head * HEAD_DIM, (head + 1) * HEAD_DIM)
        wide = slice(chunk * width + head * HEAD_DIM, chunk * width + (head + 1) * HEAD_DIM)
        query = query_ref[:, wide]
        grad = jnp.where(query_valid, grad_ref[:, wide], none)
        keys = jnp.concatenate([block[0, :, cols] for block in blocks], axis=0)
        values = jnp.concatenate([block[1, :, cols] for block in blocks], axis=0)
        scores = lax.dot_general(keys, query, nt, preferred_element_type=jnp.float32) + bias
        top = jnp.max(scores, axis=0, keepdims=True)
        expon = jnp.exp2((scores - top) * scaling_two)
        probs = expon * (1.0 / jnp.sum(expon, axis=0, keepdims=True))
        half = probs.astype(jnp.bfloat16)
        grad_probs = lax.dot_general(values, grad, nt, preferred_element_type=jnp.float32)
        row_dot = jnp.sum(probs * grad_probs, axis=0, keepdims=True)
        grad_scores = (probs * (grad_probs - row_dot)).astype(jnp.bfloat16)
        grad_value = jnp.dot(half, grad, preferred_element_type=jnp.float32).astype(jnp.bfloat16)
        grad_key = jnp.dot(grad_scores, query, preferred_element_type=jnp.float32) * scaling
        grad_key = grad_key.astype(jnp.bfloat16)
        context = lax.dot_general(values, half, tn, preferred_element_type=jnp.float32).astype(jnp.bfloat16).T
        attended_ref[:, wide] = jnp.where(query_valid, context, none)
        grad_query = lax.dot_general(keys, grad_scores, tn, preferred_element_type=jnp.float32) * scaling
        grad_query_ref[:, wide] = grad_query.astype(jnp.bfloat16).T
        for step in range(section_count):
            rows = slice(step * block_len, (step + 1) * block_len)
            outs[step][0, :, cols] = grad_key[rows]
            outs[step][1, :, cols] = grad_value[rows]


def sum_kernel(tp_count, section_count, facts_ref, *refs):
    pieces, outs = refs[:section_count], refs[section_count:]
    me, tp_me = lax.axis_index("section"), lax.axis_index("tp")
    for step in range(tp_count):
        micro = ahead(tp_me, step, tp_count)
        total = jnp.zeros(outs[step].shape, jnp.float32)
        for back in range(section_count):
            weight = jnp.where(facts_ref[me ^ back] == micro, 1.0, 0.0)
            total = total + weight * pieces[back][...].astype(jnp.float32)
        outs[step][...] = total.astype(jnp.bfloat16)


def join_kernel(tp_count, chunk, width, head_cols, *refs):
    pieces, out_ref, sem = refs[:tp_count], refs[-2], refs[-1]
    me = lax.axis_index("tp")
    owners = [behind(me, step, tp_count) for step in range(tp_count)]
    run_copies([(piece, out_ref.at[:, :, columns_of(chunk, width, head_cols, o)]) for o, piece in zip(owners, pieces)], sem)


def body(enc_kv, queries, grad_out, plan, enc_lengths, tgt_lengths):
    section_count = lax.axis_size("section")
    tp_count = lax.axis_size("tp")
    memory = enc_kv[0, :, 0]
    query, grad = queries[0, 0], grad_out[0, 0]
    block_len, columns = memory.shape[1:]
    tgt, head_cols = query.shape
    heads = head_cols // HEAD_DIM
    chunks = math.gcd(CHUNKS, heads)
    width = head_cols // chunks
    piece = pltpu.VMEM((2, block_len, width), jnp.bfloat16)
    rows = pltpu.VMEM((tgt, head_cols), jnp.bfloat16)
    params = pltpu.CompilerParams(vmem_limit_bytes=16 * 1024 * 1024)

    memory = pltpu.with_memory_space_constraint(memory, pltpu.HBM)
    copy_sem = pltpu.SemaphoreType.DMA((tp_count,))
    parts = []
    for chunk in range(chunks):
        gate = [parts[-1][2]] if parts else []
        split = pl.pallas_call(
            functools.partial(split_kernel, tp_count, chunk, width, head_cols),
            out_shape=[piece] * tp_count,
            in_specs=[ANY] * (1 + len(gate)),
            out_specs=[VMEM] * tp_count,
            scratch_shapes=[copy_sem],
            compiler_params=params,
            name=f"split{chunk}",
        )(memory, *gate)
        parts.append([split[0]] + [shift(split[step], step, tp_count) for step in range(1, tp_count)])
    facts = pl.pallas_call(
        functools.partial(facts_kernel, section_count),
        out_shape=pltpu.SMEM((section_count + 2,), jnp.int32),
        in_specs=[SMEM] * 3,
        out_specs=SMEM,
        compiler_params=params,
        name="facts",
    )(plan, enc_lengths, tgt_lengths)
    facts = pltpu.with_memory_space_constraint(facts, pltpu.SMEM)

    def pick(chunk, steps, gate):
        return pl.pallas_call(
            functools.partial(pick_kernel, tp_count, steps),
            out_shape=[piece] * len(steps),
            in_specs=[SMEM] + [VMEM] * (tp_count + len(gate)),
            out_specs=[VMEM] * len(steps),
            compiler_params=params,
            name=f"pick{chunk}",
        )(facts, *map(near, parts[chunk]), *map(near, gate))

    query, grad = near(query), near(grad)
    results, returned = [], []
    steps = list(range(section_count))
    for chunk in range(chunks):
        if chunk == 0:
            picked = pick(chunk, steps, [])
        else:
            picked = pick(chunk, steps[:-1], []) + pick(chunk, steps[-1:], [returned[-1][0]])
        arrived = [picked[0]] + [swap(picked[step], step, section_count) for step in steps[1:]]
        done = pl.pallas_call(
            functools.partial(heads_kernel, section_count, chunk, width),
            out_shape=[rows, rows] + [piece] * section_count,
            in_specs=[SMEM] + [VMEM] * (2 + section_count + len(results)),
            out_specs=[VMEM] * (2 + section_count),
            input_output_aliases={3 + section_count + i: i for i in range(len(results))},
            compiler_params=params,
            cost_estimate=pl.CostEstimate(
                flops=12 * tgt * block_len * section_count * width, bytes_accessed=8 * 2**20, transcendentals=0
            ),
            name=f"heads{chunk}",
        )(facts, query, grad, *map(near, arrived), *map(near, results))
        results = list(done[:2])
        returned.append([done[2]] + [swap(done[2 + step], step, section_count) for step in steps[1:]])

    whole = []
    for chunk in range(chunks):
        summed = pl.pallas_call(
            functools.partial(sum_kernel, tp_count, section_count),
            out_shape=[piece] * tp_count,
            in_specs=[SMEM] + [VMEM] * section_count,
            out_specs=[VMEM] * tp_count,
            compiler_params=params,
            name=f"sum{chunk}",
        )(facts, *map(near, returned[chunk]))
        pieces = [summed[0]] + [shift(summed[step], step, tp_count) for step in range(1, tp_count)]
        whole = [
            pl.pallas_call(
                functools.partial(join_kernel, tp_count, chunk, width, head_cols),
                out_shape=pltpu.HBM((2, block_len, columns), jnp.bfloat16),
                in_specs=[VMEM] * tp_count + [ANY] * len(whole),
                out_specs=ANY,
                scratch_shapes=[copy_sem],
                input_output_aliases={tp_count: 0} if whole else {},
                compiler_params=params,
                name=f"join{chunk}",
            )(*map(near, pieces), *whole)
        ]
    return (results[0][None, None], results[1][None, None], whole[0][None, :, None])


def solution(mesh):
    in_specs = (
        P("dp", None, "tp", "section", None),
        P("dp", "section", None, "tp"),
        P("dp", "section", None, "tp"),
        P("dp", None),
        P("dp", None),
        P("dp", None),
    )
    out_specs = (
        P("dp", "section", None, "tp"),
        P("dp", "section", None, "tp"),
        P("dp", None, "tp", "section", None),
    )
    return jax.shard_map(body, mesh=mesh, in_specs=in_specs, out_specs=out_specs, check_vma=False)
```

```python
import functools
import math

import jax
import jax.numpy as jnp
from jax import lax
from jax.experimental import pallas as pl
from jax.experimental.pallas import tpu as pltpu
from jax.sharding import PartitionSpec as P

HEAD_DIM = 128
CHUNKS = 2

SMEM = pl.BlockSpec(memory_space=pltpu.SMEM)
VMEM = pl.BlockSpec(memory_space=pltpu.VMEM)
ANY = pl.BlockSpec(memory_space=pl.ANY)


def ahead(index, step, count):
    return lax.rem(index + step, count)


def behind(index, step, count):
    return lax.rem(index + count - step, count)


def swap(piece, step, count):
    return lax.ppermute(piece, "section", [(i, i ^ step) for i in range(count)])


def shift(piece, step, count):
    return lax.ppermute(piece, "tp", [(i, (i + step) % count) for i in range(count)])


def near(array):
    return pltpu.with_memory_space_constraint(array, pltpu.VMEM)


def columns_of(chunk, width, head_cols, owner):
    return pl.ds(pl.multiple_of(owner * head_cols + chunk * width, 128), width)


def run_copies(pairs, sem):
    copies = [pltpu.make_async_copy(source, target, sem.at[i]) for i, (source, target) in enumerate(pairs)]
    for copy in copies:
        copy.start()
    for copy in copies:
        copy.wait()


def split_kernel(tp_count, chunk, width, head_cols, memory_ref, *refs):
    me = lax.axis_index("tp")
    outs, sem = refs[-1 - tp_count : -1], refs[-1]
    owners = [ahead(me, step, tp_count) for step in range(tp_count)]
    run_copies([(memory_ref.at[:, :, columns_of(chunk, width, head_cols, o)], out) for o, out in zip(owners, outs)], sem)


def facts_kernel(section_count, plan_ref, key_len_ref, query_len_ref, facts_ref):
    for section in range(section_count):
        facts_ref[section] = plan_ref[0, section]
    micro = plan_ref[0, lax.axis_index("section")]
    facts_ref[section_count] = key_len_ref[0, micro]
    facts_ref[section_count + 1] = query_len_ref[0, micro]


def pick_kernel(tp_count, steps, facts_ref, *refs):
    pieces, outs = refs[:tp_count], refs[-len(steps) :]
    me, tp_me = lax.axis_index("section"), lax.axis_index("tp")
    for step, out_ref in zip(steps, outs):
        back = behind(tp_me, facts_ref[me ^ step], tp_count)
        for which in range(tp_count):

            @pl.when(back == which)
            def _():
                out_ref[...] = pieces[which][...]


def heads_kernel(section_count, chunk, width, facts_ref, query_ref, grad_ref, *refs):
    blocks = refs[:section_count]
    attended_ref, grad_query_ref, *outs = refs[-2 - section_count :]
    me = lax.axis_index("section")
    key_len, query_len = facts_ref[section_count], facts_ref[section_count + 1]
    block_len = blocks[0].shape[1]
    tgt = query_ref.shape[0]
    scaling = HEAD_DIM ** (-0.5)
    scaling_two = scaling * math.log2(math.e)
    row = lax.broadcasted_iota(jnp.int32, (block_len, 1), 0)
    lefts = [key_len - (me ^ step) * block_len for step in range(section_count)]
    bias = jnp.concatenate([jnp.where(row < left, 0.0, -jnp.inf) for left in lefts], axis=0)
    query_valid = lax.broadcasted_iota(jnp.int32, (tgt, HEAD_DIM), 0) < query_len
    nt = (((1,), (1,)), ((), ()))
    tn = (((0,), (0,)), ((), ()))
    none = jnp.zeros((), jnp.bfloat16)
    heads = width // HEAD_DIM

    def load(head):
        cols = slice(head * HEAD_DIM, (head + 1) * HEAD_DIM)
        wide = slice(chunk * width + head * HEAD_DIM, chunk * width + (head + 1) * HEAD_DIM)
        query = query_ref[:, wide]
        grad = jnp.where(query_valid, grad_ref[:, wide], none)
        keys = jnp.concatenate([block[0, :, cols] for block in blocks], axis=0)
        values = jnp.concatenate([block[1, :, cols] for block in blocks], axis=0)
        scores = lax.dot_general(keys, query, nt, preferred_element_type=jnp.float32) + bias
        grad_probs = lax.dot_general(values, grad, nt, preferred_element_type=jnp.float32)
        return cols, wide, query, grad, keys, values, scores, grad_probs

    loaded = load(0)
    for head in range(heads):
        cols, wide, query, grad, keys, values, scores, grad_probs = loaded
        if head + 1 < heads:
            loaded = load(head + 1)
        top = jnp.max(scores, axis=0, keepdims=True)
        expon = jnp.exp2((scores - top) * scaling_two)
        probs = expon * (1.0 / jnp.sum(expon, axis=0, keepdims=True))
        half = probs.astype(jnp.bfloat16)
        row_dot = jnp.sum(probs * grad_probs, axis=0, keepdims=True)
        grad_scores = (probs * (grad_probs - row_dot)).astype(jnp.bfloat16)
        grad_value = jnp.dot(half, grad, preferred_element_type=jnp.float32).astype(jnp.bfloat16)
        grad_key = jnp.dot(grad_scores, query, preferred_element_type=jnp.float32) * scaling
        grad_key = grad_key.astype(jnp.bfloat16)
        context = lax.dot_general(values, half, tn, preferred_element_type=jnp.float32).astype(jnp.bfloat16).T
        attended_ref[:, wide] = jnp.where(query_valid, context, none)
        grad_query = lax.dot_general(keys, grad_scores, tn, preferred_element_type=jnp.float32) * scaling
        grad_query_ref[:, wide] = grad_query.astype(jnp.bfloat16).T
        for step in range(section_count):
            rows = slice(step * block_len, (step + 1) * block_len)
            outs[step][0, :, cols] = grad_key[rows]
            outs[step][1, :, cols] = grad_value[rows]


def sum_kernel(tp_count, section_count, facts_ref, *refs):
    pieces, outs = refs[:section_count], refs[section_count:]
    me, tp_me = lax.axis_index("section"), lax.axis_index("tp")
    for step in range(tp_count):
        micro = ahead(tp_me, step, tp_count)
        total = jnp.zeros(outs[step].shape, jnp.float32)
        for back in range(section_count):
            weight = jnp.where(facts_ref[me ^ back] == micro, 1.0, 0.0)
            total = total + weight * pieces[back][...].astype(jnp.float32)
        outs[step][...] = total.astype(jnp.bfloat16)


def join_kernel(tp_count, chunk, width, head_cols, *refs):
    pieces, out_ref, sem = refs[:tp_count], refs[-2], refs[-1]
    me = lax.axis_index("tp")
    owners = [behind(me, step, tp_count) for step in range(tp_count)]
    run_copies([(piece, out_ref.at[:, :, columns_of(chunk, width, head_cols, o)]) for o, piece in zip(owners, pieces)], sem)


def body(enc_kv, queries, grad_out, plan, enc_lengths, tgt_lengths):
    section_count = lax.axis_size("section")
    tp_count = lax.axis_size("tp")
    memory = enc_kv[0, :, 0]
    query, grad = queries[0, 0], grad_out[0, 0]
    block_len, columns = memory.shape[1:]
    tgt, head_cols = query.shape
    heads = head_cols // HEAD_DIM
    chunks = math.gcd(CHUNKS, heads)
    width = head_cols // chunks
    piece = pltpu.VMEM((2, block_len, width), jnp.bfloat16)
    rows = pltpu.VMEM((tgt, head_cols), jnp.bfloat16)
    params = pltpu.CompilerParams(vmem_limit_bytes=16 * 1024 * 1024)

    memory = pltpu.with_memory_space_constraint(memory, pltpu.HBM)
    copy_sem = pltpu.SemaphoreType.DMA((tp_count,))
    parts = []
    for chunk in range(chunks):
        gate = [parts[-1][1]] if parts else []
        split = pl.pallas_call(
            functools.partial(split_kernel, tp_count, chunk, width, head_cols),
            out_shape=[piece] * tp_count,
            in_specs=[ANY] * (1 + len(gate)),
            out_specs=[VMEM] * tp_count,
            scratch_shapes=[copy_sem],
            compiler_params=params,
            name=f"split{chunk}",
        )(memory, *gate)
        parts.append([split[0]] + [shift(split[step], step, tp_count) for step in range(1, tp_count)])
    facts = pl.pallas_call(
        functools.partial(facts_kernel, section_count),
        out_shape=pltpu.SMEM((section_count + 2,), jnp.int32),
        in_specs=[SMEM] * 3,
        out_specs=SMEM,
        compiler_params=params,
        name="facts",
    )(plan, enc_lengths, tgt_lengths)
    facts = pltpu.with_memory_space_constraint(facts, pltpu.SMEM)

    def pick(chunk, steps, gate):
        return pl.pallas_call(
            functools.partial(pick_kernel, tp_count, steps),
            out_shape=[piece] * len(steps),
            in_specs=[SMEM] + [VMEM] * (tp_count + len(gate)),
            out_specs=[VMEM] * len(steps),
            compiler_params=params,
            name=f"pick{chunk}",
        )(facts, *map(near, parts[chunk]), *map(near, gate))

    query, grad = near(query), near(grad)
    results, returned = [], []
    steps = list(range(section_count))
    for chunk in range(chunks):
        if chunk == 0:
            picked = pick(chunk, steps, [])
        else:
            picked = pick(chunk, steps[:-1], []) + pick(chunk, steps[-1:], [returned[-1][0]])
        arrived = [picked[0]] + [swap(picked[step], step, section_count) for step in steps[1:]]
        done = pl.pallas_call(
            functools.partial(heads_kernel, section_count, chunk, width),
            out_shape=[rows, rows] + [piece] * section_count,
            in_specs=[SMEM] + [VMEM] * (2 + section_count + len(results)),
            out_specs=[VMEM] * (2 + section_count),
            input_output_aliases={3 + section_count + i: i for i in range(len(results))},
            compiler_params=params,
            cost_estimate=pl.CostEstimate(
                flops=12 * tgt * block_len * section_count * width, bytes_accessed=8 * 2**20, transcendentals=0
            ),
            name=f"heads{chunk}",
        )(facts, query, grad, *map(near, arrived), *map(near, results))
        results = list(done[:2])
        returned.append([done[2]] + [swap(done[2 + step], step, section_count) for step in steps[1:]])

    whole = []
    for chunk in range(chunks):
        summed = pl.pallas_call(
            functools.partial(sum_kernel, tp_count, section_count),
            out_shape=[piece] * tp_count,
            in_specs=[SMEM] + [VMEM] * section_count,
            out_specs=[VMEM] * tp_count,
            compiler_params=params,
            name=f"sum{chunk}",
        )(facts, *map(near, returned[chunk]))
        pieces = [summed[0]] + [shift(summed[step], step, tp_count) for step in range(1, tp_count)]
        whole = [
            pl.pallas_call(
                functools.partial(join_kernel, tp_count, chunk, width, head_cols),
                out_shape=pltpu.HBM((2, block_len, columns), jnp.bfloat16),
                in_specs=[VMEM] * tp_count + [ANY] * len(whole),
                out_specs=ANY,
                scratch_shapes=[copy_sem],
                input_output_aliases={tp_count: 0} if whole else {},
                compiler_params=params,
                name=f"join{chunk}",
            )(*map(near, pieces), *whole)
        ]
    return (results[0][None, None], results[1][None, None], whole[0][None, :, None])


def solution(mesh):
    in_specs = (
        P("dp", None, "tp", "section", None),
        P("dp", "section", None, "tp"),
        P("dp", "section", None, "tp"),
        P("dp", None),
        P("dp", None),
        P("dp", None),
    )
    out_specs = (
        P("dp", "section", None, "tp"),
        P("dp", "section", None, "tp"),
        P("dp", None, "tp", "section", None),
    )
    return jax.shard_map(body, mesh=mesh, in_specs=in_specs, out_specs=out_specs, check_vma=False)
```

```python
import functools
import math

import jax
import jax.numpy as jnp
from jax import lax
from jax.experimental import pallas as pl
from jax.experimental.pallas import tpu as pltpu
from jax.sharding import PartitionSpec as P

HEAD_DIM = 128
CHUNKS = 2

SMEM = pl.BlockSpec(memory_space=pltpu.SMEM)
VMEM = pl.BlockSpec(memory_space=pltpu.VMEM)
ANY = pl.BlockSpec(memory_space=pl.ANY)


def ahead(index, step, count):
    return lax.rem(index + step, count)


def behind(index, step, count):
    return lax.rem(index + count - step, count)


def swap(piece, step, count):
    return lax.ppermute(piece, "section", [(i, i ^ step) for i in range(count)])


def shift(piece, step, count):
    return lax.ppermute(piece, "tp", [(i, (i + step) % count) for i in range(count)])


def near(array):
    return pltpu.with_memory_space_constraint(array, pltpu.VMEM)


def columns_of(chunk, width, head_cols, owner):
    return pl.ds(pl.multiple_of(owner * head_cols + chunk * width, 128), width)


def run_copies(pairs, sem):
    copies = [pltpu.make_async_copy(source, target, sem.at[i]) for i, (source, target) in enumerate(pairs)]
    for copy in copies:
        copy.start()
    for copy in copies:
        copy.wait()


def split_kernel(tp_count, chunk, width, head_cols, memory_ref, *refs):
    me = lax.axis_index("tp")
    outs, sem = refs[-1 - tp_count : -1], refs[-1]
    owners = [ahead(me, step, tp_count) for step in range(tp_count)]
    run_copies([(memory_ref.at[:, :, columns_of(chunk, width, head_cols, o)], out) for o, out in zip(owners, outs)], sem)


def first_split_kernel(tp_count, chunk, width, head_cols, memory_ref, plan_in, key_len_in, query_len_in, facts_ref, *refs):
    outs, (plan_ref, key_len_ref, query_len_ref, sem) = refs[:tp_count], refs[tp_count:]
    me = lax.axis_index("tp")
    section_count = plan_ref.shape[1]
    owners = [ahead(me, step, tp_count) for step in range(tp_count)]
    pairs = [(memory_ref.at[:, :, columns_of(chunk, width, head_cols, o)], out) for o, out in zip(owners, outs)]
    scalars = [(plan_in, plan_ref), (key_len_in, key_len_ref), (query_len_in, query_len_ref)]
    run_copies(pairs + scalars, sem)
    for section in range(section_count):
        facts_ref[section] = plan_ref[0, section]
    micro = plan_ref[0, lax.axis_index("section")]
    facts_ref[section_count] = key_len_ref[0, micro]
    facts_ref[section_count + 1] = query_len_ref[0, micro]


def pick_kernel(tp_count, steps, facts_ref, *refs):
    pieces, outs = refs[:tp_count], refs[-len(steps) :]
    me, tp_me = lax.axis_index("section"), lax.axis_index("tp")
    for step, out_ref in zip(steps, outs):
        back = behind(tp_me, facts_ref[me ^ step], tp_count)
        for which in range(tp_count):

            @pl.when(back == which)
            def _():
                out_ref[...] = pieces[which][...]


def heads_kernel(section_count, chunk, width, facts_ref, query_ref, grad_ref, *refs):
    blocks = refs[:section_count]
    attended_ref, grad_query_ref, *outs = refs[-2 - section_count :]
    me = lax.axis_index("section")
    key_len, query_len = facts_ref[section_count], facts_ref[section_count + 1]
    block_len = blocks[0].shape[1]
    tgt = query_ref.shape[0]
    scaling = HEAD_DIM ** (-0.5)
    scaling_two = scaling * math.log2(math.e)
    row = lax.broadcasted_iota(jnp.int32, (block_len, 1), 0)
    lefts = [key_len - (me ^ step) * block_len for step in range(section_count)]
    bias = jnp.concatenate([jnp.where(row < left, 0.0, -jnp.inf) for left in lefts], axis=0)
    query_valid = lax.broadcasted_iota(jnp.int32, (tgt, HEAD_DIM), 0) < query_len
    nt = (((1,), (1,)), ((), ()))
    tn = (((0,), (0,)), ((), ()))
    none = jnp.zeros((), jnp.bfloat16)
    heads = width // HEAD_DIM

    def load(head):
        cols = slice(head * HEAD_DIM, (head + 1) * HEAD_DIM)
        wide = slice(chunk * width + head * HEAD_DIM, chunk * width + (head + 1) * HEAD_DIM)
        query = query_ref[:, wide]
        grad = jnp.where(query_valid, grad_ref[:, wide], none)
        keys = jnp.concatenate([block[0, :, cols] for block in blocks], axis=0)
        values = jnp.concatenate([block[1, :, cols] for block in blocks], axis=0)
        scores = lax.dot_general(keys, query, nt, preferred_element_type=jnp.float32) + bias
        grad_probs = lax.dot_general(values, grad, nt, preferred_element_type=jnp.float32)
        return cols, wide, query, grad, keys, values, scores, grad_probs

    loaded = load(0)
    for head in range(heads):
        cols, wide, query, grad, keys, values, scores, grad_probs = loaded
        if head + 1 < heads:
            loaded = load(head + 1)
        top = jnp.max(scores, axis=0, keepdims=True)
        expon = jnp.exp2((scores - top) * scaling_two)
        probs = expon * (1.0 / jnp.sum(expon, axis=0, keepdims=True))
        half = probs.astype(jnp.bfloat16)
        row_dot = jnp.sum(probs * grad_probs, axis=0, keepdims=True)
        grad_scores = (probs * (grad_probs - row_dot)).astype(jnp.bfloat16)
        grad_value = jnp.dot(half, grad, preferred_element_type=jnp.float32).astype(jnp.bfloat16)
        grad_key = jnp.dot(grad_scores, query, preferred_element_type=jnp.float32) * scaling
        grad_key = grad_key.astype(jnp.bfloat16)
        context = lax.dot_general(values, half, tn, preferred_element_type=jnp.float32).astype(jnp.bfloat16).T
        attended_ref[:, wide] = jnp.where(query_valid, context, none)
        grad_query = lax.dot_general(keys, grad_scores, tn, preferred_element_type=jnp.float32) * scaling
        grad_query_ref[:, wide] = grad_query.astype(jnp.bfloat16).T
        for step in range(section_count):
            rows = slice(step * block_len, (step + 1) * block_len)
            outs[step][0, :, cols] = grad_key[rows]
            outs[step][1, :, cols] = grad_value[rows]


def sum_kernel(tp_count, section_count, facts_ref, *refs):
    pieces, outs = refs[:section_count], refs[section_count:]
    me, tp_me = lax.axis_index("section"), lax.axis_index("tp")
    for step in range(tp_count):
        micro = ahead(tp_me, step, tp_count)
        total = jnp.zeros(outs[step].shape, jnp.float32)
        for back in range(section_count):
            weight = jnp.where(facts_ref[me ^ back] == micro, 1.0, 0.0)
            total = total + weight * pieces[back][...].astype(jnp.float32)
        outs[step][...] = total.astype(jnp.bfloat16)


def join_kernel(tp_count, chunk, width, head_cols, *refs):
    pieces, out_ref, sem = refs[:tp_count], refs[-2], refs[-1]
    me = lax.axis_index("tp")
    owners = [behind(me, step, tp_count) for step in range(tp_count)]
    run_copies([(piece, out_ref.at[:, :, columns_of(chunk, width, head_cols, o)]) for o, piece in zip(owners, pieces)], sem)


def body(enc_kv, queries, grad_out, plan, enc_lengths, tgt_lengths):
    section_count = lax.axis_size("section")
    tp_count = lax.axis_size("tp")
    memory = enc_kv[0, :, 0]
    query, grad = queries[0, 0], grad_out[0, 0]
    block_len, columns = memory.shape[1:]
    tgt, head_cols = query.shape
    heads = head_cols // HEAD_DIM
    chunks = math.gcd(CHUNKS, heads)
    width = head_cols // chunks
    piece = pltpu.VMEM((2, block_len, width), jnp.bfloat16)
    rows = pltpu.VMEM((tgt, head_cols), jnp.bfloat16)
    params = pltpu.CompilerParams(vmem_limit_bytes=16 * 1024 * 1024)

    memory = pltpu.with_memory_space_constraint(memory, pltpu.HBM)
    copy_sem = pltpu.SemaphoreType.DMA((tp_count,))
    scalars = [pltpu.with_memory_space_constraint(array, pltpu.HBM) for array in (plan, enc_lengths, tgt_lengths)]
    facts, *split = pl.pallas_call(
        functools.partial(first_split_kernel, tp_count, 0, width, head_cols),
        out_shape=[pltpu.SMEM((section_count + 2,), jnp.int32)] + [piece] * tp_count,
        in_specs=[ANY] * 4,
        out_specs=[SMEM] + [VMEM] * tp_count,
        scratch_shapes=[pltpu.SMEM(array.shape, jnp.int32) for array in (plan, enc_lengths, tgt_lengths)]
        + [pltpu.SemaphoreType.DMA((tp_count + 3,))],
        compiler_params=params,
        name="split0",
    )(memory, *scalars)
    parts = [[split[0]] + [shift(split[step], step, tp_count) for step in range(1, tp_count)]]
    for chunk in range(1, chunks):
        gate = [parts[-1][1]]
        split = pl.pallas_call(
            functools.partial(split_kernel, tp_count, chunk, width, head_cols),
            out_shape=[piece] * tp_count,
            in_specs=[ANY] * (1 + len(gate)),
            out_specs=[VMEM] * tp_count,
            scratch_shapes=[copy_sem],
            compiler_params=params,
            name=f"split{chunk}",
        )(memory, *gate)
        parts.append([split[0]] + [shift(split[step], step, tp_count) for step in range(1, tp_count)])
    facts = pltpu.with_memory_space_constraint(facts, pltpu.SMEM)

    def pick(chunk, steps, gate):
        return pl.pallas_call(
            functools.partial(pick_kernel, tp_count, steps),
            out_shape=[piece] * len(steps),
            in_specs=[SMEM] + [VMEM] * (tp_count + len(gate)),
            out_specs=[VMEM] * len(steps),
            compiler_params=params,
            name=f"pick{chunk}",
        )(facts, *map(near, parts[chunk]), *map(near, gate))

    query, grad = near(query), near(grad)
    results, returned = [], []
    steps = list(range(section_count))
    for chunk in range(chunks):
        if chunk == 0:
            picked = pick(chunk, steps, [])
        else:
            picked = pick(chunk, steps[:-1], []) + pick(chunk, steps[-1:], [returned[-1][0]])
        arrived = [picked[0]] + [swap(picked[step], step, section_count) for step in steps[1:]]
        done = pl.pallas_call(
            functools.partial(heads_kernel, section_count, chunk, width),
            out_shape=[rows, rows] + [piece] * section_count,
            in_specs=[SMEM] + [VMEM] * (2 + section_count + len(results)),
            out_specs=[VMEM] * (2 + section_count),
            input_output_aliases={3 + section_count + i: i for i in range(len(results))},
            compiler_params=params,
            cost_estimate=pl.CostEstimate(
                flops=12 * tgt * block_len * section_count * width, bytes_accessed=8 * 2**20, transcendentals=0
            ),
            name=f"heads{chunk}",
        )(facts, query, grad, *map(near, arrived), *map(near, results))
        results = list(done[:2])
        returned.append([done[2]] + [swap(done[2 + step], step, section_count) for step in steps[1:]])

    whole = []
    for chunk in range(chunks):
        summed = pl.pallas_call(
            functools.partial(sum_kernel, tp_count, section_count),
            out_shape=[piece] * tp_count,
            in_specs=[SMEM] + [VMEM] * section_count,
            out_specs=[VMEM] * tp_count,
            compiler_params=params,
            name=f"sum{chunk}",
        )(facts, *map(near, returned[chunk]))
        pieces = [summed[0]] + [shift(summed[step], step, tp_count) for step in range(1, tp_count)]
        whole = [
            pl.pallas_call(
                functools.partial(join_kernel, tp_count, chunk, width, head_cols),
                out_shape=pltpu.HBM((2, block_len, columns), jnp.bfloat16),
                in_specs=[VMEM] * tp_count + [ANY] * len(whole),
                out_specs=ANY,
                scratch_shapes=[copy_sem],
                input_output_aliases={tp_count: 0} if whole else {},
                compiler_params=params,
                name=f"join{chunk}",
            )(*map(near, pieces), *whole)
        ]
    return (results[0][None, None], results[1][None, None], whole[0][None, :, None])


def solution(mesh):
    in_specs = (
        P("dp", None, "tp", "section", None),
        P("dp", "section", None, "tp"),
        P("dp", "section", None, "tp"),
        P("dp", None),
        P("dp", None),
        P("dp", None),
    )
    out_specs = (
        P("dp", "section", None, "tp"),
        P("dp", "section", None, "tp"),
        P("dp", None, "tp", "section", None),
    )
    return jax.shard_map(body, mesh=mesh, in_specs=in_specs, out_specs=out_specs, check_vma=False)
```
